32 devices in a mesh: grp: 4 (over y, x), cell: 8 (over z, core).
Axes of the slice: x: 2, y: 2, z: 4, core: 2. Of those that a mesh axis runs over, the one named last changes fastest.
Arguments:
- expression: bfloat16 [2000, 16384], P(None, ('grp', 'cell')), may hold values from 0.019897461 to 4
- dataset_id: int32 [16384], P(('grp', 'cell')), may hold values from 0 to 3, as said below
- dataset_map: int32 [4], P('grp'), may hold values from 0 to 3, as said below
- sweep_count: int32 [4], replicated, may hold values from 2 to 4
- picks: int32 [2, 4096], P(None, ('grp', 'cell')), may hold values from 0 to 511
- shared_init: float32 [64, 2000], replicated, may hold values from 0.004 to 0.06
- specific_init: float32 [4, 64, 2000], P('grp'), may hold values from 0.001 to 0.02
Outputs:
- loadings: float32 [2, 64, 4096], P(None, None, ('grp', 'cell'))
- shared_basis: float32 [64, 2000], replicated
- specific_basis: float32 [4, 64, 2000], P('grp')
The draws below stay inside these ranges and needn't reach their ends.
Inputs may be any that keep to these rules, and one draw needn't show every extreme that they name: `dataset_map`: a permutation of the datasets; entry g is the one dataset of device group g. `dataset_id`: every cell held by the devices of group g belongs to one of the datasets that dataset_map gives to group g. `picks`: an index into the cells held by the device that holds the slot; a cell may be picked more than once.
All inputs are finite; a program needn't handle non-finite values.
Results may differ from the reference program's by a relative error of at most 0.0065.
The reference program's roundings to bfloat16 on the way count: a program that leaves them out, or rounds other values in their place, can miss the bound.
Values sent between devices are 32-bit elements; how exact they have to be, the bound alone decides.
A program may use at most 128 MiB of HBM per device.

```python
import math
import jax
import jax.numpy as jnp
from jax import lax

G = 2000
K = 64
SWEEPS = 4
ROUNDS = 2
DS_GRP = 1
CELLS_DEV = 128
POOL_DEV = 512
DATASETS = 4
CELLS = 4096
POOL = 16384
N_GRP = 4
N_CELL = 8


def map_and_slots(key):
    base_key = jax.random.fold_in(key, 7001)
    dataset_order = jax.random.permutation(jax.random.fold_in(base_key, 1), DATASETS).astype(jnp.int32)
    first_pick = jax.random.randint(jax.random.fold_in(base_key, 2), (POOL,), 0, DS_GRP)
    second = jax.random.randint(jax.random.fold_in(base_key, 3), (POOL,), 0, DS_GRP)
    slot_pick = jnp.minimum(first_pick, second)
    group_of = jnp.arange(POOL, dtype=jnp.int32) // (POOL_DEV * N_CELL)
    identities = dataset_order[group_of * DS_GRP + slot_pick]
    return (dataset_order, identities.astype(jnp.int32))


def draw_dataset_map(key, part):
    return map_and_slots(key)[0]


def draw_dataset_id(key, part):
    return map_and_slots(key)[1]


def with_ends(entries, own_key, least, top_value):
    shape = entries.shape
    place = [jax.random.randint(jax.random.fold_in(own_key, axis), (), 0, shape[axis]) for axis in range(len(shape))]
    entries = entries.at[tuple(place)].set(least)
    longest = shape.index(max(shape))
    place[longest] = (place[longest] + 1) % shape[longest]
    return entries.at[tuple(place)].set(top_value)


def level_of(own_key, shape, cuts, smallest, largest):
    level = 1.0
    for axis_at, blocks in cuts:
        steps = jax.random.uniform(jax.random.fold_in(jax.random.fold_in(own_key, 6), axis_at), (blocks,), jnp.float32, smallest / len(cuts), largest / len(cuts))
        level = level * jnp.repeat(jnp.exp(steps), shape[axis_at] // blocks).reshape((-1,) + (1,) * (len(shape) - 1 - axis_at))
    return level


def setup_inputs(seed: int = 0) -> dict:
    key_of = jax.random.split(jax.random.key(seed), 8)
    return {
        "expression": jnp.clip(jnp.exp(math.log(4.0) - 5.3034575 * jax.random.uniform(key_of[0], (G, POOL), jnp.float32) ** level_of(key_of[0], (G, POOL), ((1, 32),), -0.2, 0.2)), 0.019897461, 4.0).astype(jnp.bfloat16),
        "dataset_id": draw_dataset_id(jax.random.fold_in(key_of[7], 71), 0),
        "dataset_map": draw_dataset_map(jax.random.fold_in(key_of[7], 71), 0),
        "sweep_count": with_ends(jax.random.randint(key_of[3], (DATASETS,), 2, SWEEPS + 1), jax.random.fold_in(key_of[3], 1), 2, SWEEPS).astype(jnp.int32),
        "picks": with_ends(jax.random.randint(key_of[4], (ROUNDS, CELLS), 0, POOL_DEV), jax.random.fold_in(key_of[4], 1), 0, POOL_DEV - 1).astype(jnp.int32),
        "shared_init": jnp.clip(jnp.exp(jax.random.uniform(key_of[5], (K, G), jnp.float32, math.log(0.004), math.log(0.06))), 0.004, 0.06),
        "specific_init": jnp.clip(jnp.exp(math.log(0.02) - 2.9957322 * jax.random.uniform(key_of[6], (DATASETS, K, G), jnp.float32) ** level_of(key_of[6], (DATASETS, K, G), ((0, 4),), -0.2, 0.2)), 0.001, 0.02),
    }


EPSILON = 1e-6
LAMBDA = 5.0
HIGHEST = lax.Precision.HIGHEST


def hals_loadings(target, gram_matrix, member, counts):
    divisor = jnp.einsum("jk,jn->kn", jnp.diagonal(gram_matrix, axis1=1, axis2=2) + EPSILON, member, precision=HIGHEST)

    def sweep(sweep_index, current):
        active = sweep_index < counts
        for factor in range(K):
            row_terms = jnp.einsum("jl,ln->jn", gram_matrix[:, factor, :], current, precision=HIGHEST)
            product = jnp.sum(row_terms * member, axis=0)
            updated = jnp.maximum(current[factor] + (target[factor] - product) / divisor[factor], 0.0)
            current = current.at[factor].set(jnp.where(active, updated, current[factor]))
        return current

    return lax.fori_loop(0, SWEEPS, sweep, jnp.zeros(target.shape, jnp.float32))


def solve_loadings(cell_data, member, counts, shared, specific):
    combined = shared[None] + specific
    slot_total = specific.shape[0]
    stacked = combined.astype(jnp.bfloat16).reshape(slot_total * K, combined.shape[2])
    target = jnp.dot(stacked, cell_data, preferred_element_type=jnp.float32)
    target = jnp.sum(target.reshape(slot_total, K, cell_data.shape[1]) * member[:, None, :], axis=0)
    gram_matrix = jnp.einsum("jkg,jlg->jkl", combined, combined, precision=HIGHEST) + LAMBDA * jnp.einsum("jkg,jlg->jkl", specific, specific, precision=HIGHEST)
    return hals_loadings(target, gram_matrix, member, counts)


def renew_shared(shared, gram_total, carried):
    for factor in range(K):
        change = (carried[factor] - jnp.dot(gram_total[factor], shared, precision=HIGHEST)) / jnp.maximum(gram_total[factor, factor], 1.0)
        shared = shared.at[factor].set(jnp.maximum(shared[factor] + change, 0.0))
    return shared


def renew_specific(specific, shared, gram_sets, stat_sets):
    for factor in range(K):
        weights = gram_sets[:, factor, :]
        pulled = jnp.dot(weights, shared, precision=HIGHEST) + (1.0 + LAMBDA) * jnp.einsum("sl,slg->sg", weights, specific, precision=HIGHEST)
        divisor = jnp.maximum((1.0 + LAMBDA) * gram_sets[:, factor, factor], 1.0)
        updated = jnp.maximum(specific[:, factor] + (stat_sets[:, factor] - pulled) / divisor[:, None], 0.0)
        specific = specific.at[:, factor].set(updated)
    return specific


def reference(expression, dataset_id, dataset_map, sweep_count, picks, shared_init, specific_init):
    group_width = CELLS_DEV * N_CELL
    listing = jnp.arange(DATASETS, dtype=jnp.int32)
    slot_sweeps = jnp.sum(jnp.where(dataset_map[:, None] == listing[None, :], sweep_count[None, :], 0), axis=1).astype(jnp.int32)
    device_of = jnp.arange(CELLS, dtype=jnp.int32) // CELLS_DEV
    group_of = device_of // N_CELL
    group_slots = dataset_map.reshape(N_GRP, DS_GRP)[group_of]
    group_sweeps = slot_sweeps.reshape(N_GRP, DS_GRP)[group_of]
    basis_list = [(shared_init, specific_init)]
    gram_sets = jnp.zeros((DATASETS, K, K), jnp.float32)
    stat_sets = jnp.zeros((DATASETS, K, G), jnp.float32)
    gram_total = jnp.zeros((K, K), jnp.float32)
    results = []
    for round_index in range(ROUNDS):
        pool_index = (device_of * POOL_DEV + picks[round_index]).astype(jnp.int32)
        cell_data = jnp.take(expression, pool_index, axis=1)
        matches = group_slots == dataset_id[pool_index][:, None]
        member = matches.astype(jnp.float32).T
        counts = jnp.sum(jnp.where(matches, group_sweeps, 0), axis=1).astype(jnp.int32)
        shared_use, specific_use = basis_list[max(round_index - 1, 0)]
        grouped_data = cell_data.reshape(G, N_GRP, group_width).transpose(1, 0, 2)
        grouped_member = member.reshape(DS_GRP, N_GRP, group_width).transpose(1, 0, 2)
        grouped_counts = counts.reshape(N_GRP, group_width)
        grouped_specific = specific_use.reshape(N_GRP, DS_GRP, K, G)

        def one_group(items):
            return solve_loadings(items[0], items[1], items[2], shared_use, items[3])

        grouped_loads = lax.map(one_group, (grouped_data, grouped_member, grouped_counts, grouped_specific))
        results.append(grouped_loads.transpose(1, 0, 2).reshape(K, CELLS))
        masked = grouped_loads[:, None] * grouped_member[:, :, None]
        rounded = lax.optimization_barrier(grouped_loads.astype(jnp.bfloat16)).astype(jnp.float32)
        rounded = rounded[:, None] * grouped_member[:, :, None]
        stat_round = jnp.einsum("ajkn,agn->ajkg", rounded, grouped_data.astype(jnp.float32), precision=HIGHEST)
        gram_round = jnp.einsum("ajkn,aln->ajkl", masked, grouped_loads, precision=HIGHEST)
        gram_sets = gram_sets + gram_round.reshape(DATASETS, K, K)
        stat_sets = stat_sets + stat_round.reshape(DATASETS, K, G)
        gram_total = gram_total + jnp.sum(gram_round, axis=(0, 1))
        shared_prev, specific_prev = basis_list[-1]
        carried = jnp.sum(stat_sets, axis=0) - jnp.einsum("jkl,jlg->kg", gram_sets, specific_prev, precision=HIGHEST)
        shared_next = renew_shared(shared_prev, gram_total, carried)
        specific_next = renew_specific(specific_prev, shared_next, gram_sets, stat_sets)
        basis_list.append((shared_next, specific_next))
    return jnp.stack(results), basis_list[-1][0], basis_list[-1][1]
```

```python
import functools

import jax
import jax.numpy as jnp
from jax import lax
from jax.experimental import pallas as pl
from jax.experimental.pallas import tpu as pltpu
from jax.sharding import PartitionSpec as P

K = 64
SWEEPS = 4
LANES = 128
BLOCK = 8

EPSILON = 1e-06
LAMBDA = 5.0
HIGHEST = lax.Precision.HIGHEST
MESH = pl.DeviceIdType.MESH
TRANSPOSED = (((1,), (1,)), ((), ()))


def identity_of(rows, columns):
    return (
        lax.broadcasted_iota(jnp.int32, (rows, columns), 0)
        == lax.broadcasted_iota(jnp.int32, (rows, columns), 1)
    ).astype(jnp.float32)


def cell_kernel(
    scalars, expression, picks, shared, specific,
    loadings_out, stats_out, grams_out, shared_out, specific_out,
    table, padded,
):
    rounds, chunks, _, width = stats_out.shape
    genes = shared.shape[1]
    pool = expression.shape[1]
    cells = picks.shape[1]
    per_round = cells // rounds

    padded[...] = jnp.zeros_like(padded)
    own = pl.ds(pl.multiple_of(scalars[1] * width, LANES), width)
    for source, place in ((shared, shared_out), (specific, specific_out)):
        padded[:, :genes] = source[...]
        place[...] = padded[:, own]

    combined = shared[...] + specific[...]
    gram = lax.dot_general(
        combined, combined, TRANSPOSED, precision=HIGHEST, preferred_element_type=jnp.float32
    ) + LAMBDA * lax.dot_general(
        specific[...], specific[...], TRANSPOSED, precision=HIGHEST,
        preferred_element_type=jnp.float32,
    )
    chosen = (
        lax.broadcasted_iota(jnp.int32, (pool, cells), 0) == picks[...]
    ).astype(jnp.bfloat16)
    data = jnp.dot(expression[...], chosen, preferred_element_type=jnp.float32).astype(jnp.bfloat16)
    target = jnp.dot(combined.astype(jnp.bfloat16), data, preferred_element_type=jnp.float32)

    eye = identity_of(K, K)
    divisor = jnp.sum(gram * eye, axis=1, keepdims=True) + EPSILON
    pull = eye - gram / divisor
    for factor in range(K):
        table[factor] = jnp.broadcast_to(pull[:, factor : factor + 1], (K, LANES))
    start = target / divisor
    blocks = K // BLOCK
    tiles = cells // LANES
    row = lax.broadcasted_iota(jnp.int32, (BLOCK, LANES), 0)

    def sweep(_, state):
        wish, held = [list(part) for part in state]
        for factor in range(K):
            block, place = divmod(factor, BLOCK)
            for tile in range(tiles):
                at = block * tiles + tile
                renewed = jnp.maximum(wish[at], 0.0)
                change = renewed - held[at]
                change = jnp.broadcast_to(change[place : place + 1], (BLOCK, LANES))
                held[at] = jnp.where(row == place, renewed, held[at])
                for other in range(blocks):
                    to = other * tiles + tile
                    wish[to] = (
                        wish[to]
                        + table[factor, other * BLOCK : (other + 1) * BLOCK, :] * change
                    )
        return tuple(wish), tuple(held)

    first = tuple(
        start[block * BLOCK : (block + 1) * BLOCK, tile * LANES : (tile + 1) * LANES]
        for block in range(blocks)
        for tile in range(tiles)
    )
    zero = tuple(jnp.zeros((BLOCK, LANES), jnp.float32) for _ in first)
    _, held = lax.fori_loop(0, jnp.minimum(scalars[0], SWEEPS), sweep, (first, zero))

    per_tile = per_round // LANES
    for round_index in range(rounds):
        parts = [
            jnp.concatenate([held[block * tiles + tile] for block in range(blocks)], axis=0)
            for tile in range(round_index * per_tile, (round_index + 1) * per_tile)
        ]
        loads = parts[0] if per_tile == 1 else jnp.concatenate(parts, axis=1)
        loadings_out[round_index] = loads
        grams_out[round_index] = jnp.zeros((K, LANES), jnp.float32)
        grams_out[round_index, :, :K] = lax.dot_general(
            loads, loads, TRANSPOSED, precision=HIGHEST, preferred_element_type=jnp.float32
        )
        stats = lax.dot_general(
            loads.astype(jnp.bfloat16),
            data[:, round_index * per_round : (round_index + 1) * per_round],
            TRANSPOSED,
            preferred_element_type=jnp.float32,
        )
        for chunk in range(chunks):
            low = chunk * width
            high = min(low + width, genes)
            if high < low + width:
                stats_out[round_index, chunk] = jnp.zeros((K, width), jnp.float32)
            if high > low:
                stats_out[round_index, chunk, :, : high - low] = stats[:, low:high]


def renew(current, residual, gram, scale, wish_ref, pull_ref, out_ref):
    width = current.shape[1]
    eye = identity_of(K, LANES)
    scaled = scale * gram
    divisor = jnp.maximum(jnp.sum(scaled * eye, axis=1, keepdims=True), 1.0)
    pull = eye - scaled / divisor
    wish_ref[...] = current + residual / divisor
    out_ref[...] = current
    row = lax.broadcasted_iota(jnp.int32, (BLOCK, width), 0)

    def step(block, carry):
        turned = pltpu.roll(pull, LANES - BLOCK * block, axis=1)
        pull_ref[...] = turned
        rows = pl.ds(pl.multiple_of(block * BLOCK, BLOCK), BLOCK)
        near = pull_ref[rows, :]
        wish = wish_ref[rows, :]
        held = out_ref[rows, :]
        total = wish_ref[...]
        for place in range(BLOCK):
            renewed = jnp.maximum(wish, 0.0)
            change = jnp.broadcast_to((renewed - held)[place : place + 1], (BLOCK, width))
            held = jnp.where(row == place, renewed, held)
            wish = wish + jnp.broadcast_to(near[:, place : place + 1], (BLOCK, width)) * change
            wide = jnp.concatenate([change] * (K // BLOCK), axis=0)
            total = total + jnp.broadcast_to(turned[:, place : place + 1], (K, width)) * wide
        wish_ref[...] = total
        out_ref[rows, :] = held
        return carry

    lax.fori_loop(0, K // BLOCK, step, 0)


def basis_kernel(
    groups, cell_count, stats, grams, shared, specific, shared_out, specific_out,
    sib_stats, sib_grams, along, arrived, sent, gathered, wide_shared, wide_specific,
    wish_ref, pull_ref, shared_ref, specific_ref,
    sib_send, sib_recv, along_send, along_recv, grp_send, grp_recv,
    out_send, out_recv, pair_send, pair_recv,
):
    rounds, chunks, _, width = stats.shape
    layers = cell_count // 2
    grp = lax.axis_index("grp")
    cell = lax.axis_index("cell")
    layer = cell // 2
    core = cell % 2
    sibling = layer * 2 + (1 - core)
    mine = core * layers + layer

    def layer_at(offset):
        return (layer + offset) % layers

    barrier = pltpu.get_barrier_semaphore()
    pl.semaphore_signal(barrier, inc=1, device_id={"cell": sibling}, device_id_type=MESH)
    for offset in range(1, layers):
        pl.semaphore_signal(
            barrier, inc=1, device_id={"cell": layer_at(offset) * 2 + core}, device_id_type=MESH
        )
    for offset in range(1, groups):
        pl.semaphore_signal(
            barrier, inc=1, device_id={"grp": (grp + offset) % groups}, device_id_type=MESH
        )
    pl.semaphore_wait(barrier, 1 + (layers - 1) + (groups - 1))

    started = []

    def send(source, place, send_sem, recv_sem, device):
        copy = pltpu.make_async_remote_copy(
            src_ref=source, dst_ref=place, send_sem=send_sem, recv_sem=recv_sem,
            device_id=device, device_id_type=MESH,
        )
        copy.start()
        started.append(copy)
        return copy

    pair = []
    for r in range(rounds):
        pair.append((
            send(grams.at[r], sib_grams.at[r], sib_send.at[r, 0], sib_recv.at[r, 0],
                 {"cell": sibling}),
            send(stats.at[r, pl.ds((1 - core) * layers, layers)], sib_stats.at[r],
                 sib_send.at[r, 1], sib_recv.at[r, 1], {"cell": sibling}),
        ))

    across = []
    for r in range(rounds):
        for copy in pair[r]:
            copy.wait_recv()
        gram_sum = grams[r] + sib_grams[r]
        copies = []
        for offset in range(layers - 1, -1, -1):
            at = layer_at(offset)
            along[r, offset, :, :width] = stats[r, core * layers + at] + sib_stats[r, at]
            along[r, offset, :, width:] = gram_sum
            if offset:
                copies.append(send(
                    along.at[r, offset], arrived.at[r, offset - 1],
                    along_send.at[r, offset - 1], along_recv.at[r, offset - 1],
                    {"cell": at * 2 + core},
                ))
        across.append(copies)

    shared_ref[...] = shared[...]
    specific_ref[...] = specific[...]
    stat_sum = None
    for r in range(rounds):
        for copy in across[r]:
            copy.wait_recv()
        increase = along[r, 0]
        for offset in range(1, layers):
            increase = increase + arrived[r, offset - 1]
        stat_sum = increase if stat_sum is None else stat_sum + increase
        stat, gram = stat_sum[:, :width], stat_sum[:, width:]
        small = gram[:, :K]
        before = specific_ref[...]
        pulled = jnp.dot(small, before, precision=HIGHEST, preferred_element_type=jnp.float32)
        sent[r, :, :width] = stat - pulled
        sent[r, :, width:] = gram
        copies = [
            send(sent.at[r], gathered.at[r, offset - 1], grp_send.at[r, offset - 1],
                 grp_recv.at[r, offset - 1], {"grp": (grp + offset) % groups})
            for offset in range(1, groups)
        ]
        for copy in copies:
            copy.wait_recv()
        total = sent[r]
        for offset in range(1, groups):
            total = total + gathered[r, offset - 1]
        carried, gram_total = total[:, :width], total[:, width:]
        old = shared_ref[...]
        residual = carried - jnp.dot(
            gram_total[:, :K], old, precision=HIGHEST, preferred_element_type=jnp.float32
        )
        renew(old, residual, gram_total, 1.0, wish_ref, pull_ref, shared_ref)
        last = r == rounds - 1
        if last:
            wide_shared[mine] = shared_ref[...]
            shared_copies = spread(
                send, wide_shared, 0, mine, core, layers, layer_at, sibling,
                out_send, out_recv, pair_send, pair_recv,
            )
        residual = stat - (1.0 + LAMBDA) * pulled - jnp.dot(
            small, shared_ref[...], precision=HIGHEST, preferred_element_type=jnp.float32
        )
        renew(before, residual, gram, 1.0 + LAMBDA, wish_ref, pull_ref, specific_ref)
        if last:
            wide_specific[mine] = specific_ref[...]
            specific_copies = spread(
                send, wide_specific, 1, mine, core, layers, layer_at, sibling,
                out_send, out_recv, pair_send, pair_recv,
            )

    waiting = []
    for index, (wide, copies) in enumerate(
        ((wide_shared, shared_copies), (wide_specific, specific_copies))
    ):
        fetched = [copies[0]]
        for offset in range(1, layers):
            copies[offset].wait_recv()
            came = core * layers + layer_at(layers - offset)
            fetched.append(send(
                wide.at[came], wide.at[came], pair_send.at[index, offset],
                pair_recv.at[index, offset], {"cell": sibling},
            ))
        waiting.append(fetched)
    genes = shared_out.shape[1]
    for wide, fetched, out in (
        (wide_shared, waiting[0], shared_out), (wide_specific, waiting[1], specific_out)
    ):
        for copy in fetched:
            copy.wait_recv()
        for chunk in range(chunks):
            low = chunk * width
            high = min(low + width, genes)
            if high > low:
                out[:, low:high] = wide[chunk, :, : high - low]
    for copy in started:
        copy.wait_send()


def spread(
    send, wide, index, mine, core, layers, layer_at, sibling,
    out_send, out_recv, pair_send, pair_recv,
):
    copies = {}
    for offset in range(layers - 1, 0, -1):
        copies[offset] = send(
            wide.at[mine], wide.at[mine], out_send.at[index, offset - 1],
            out_recv.at[index, offset - 1], {"cell": layer_at(offset) * 2 + core},
        )
    copies[0] = send(
        wide.at[mine], wide.at[mine], pair_send.at[index, 0], pair_recv.at[index, 0],
        {"cell": sibling},
    )
    return copies


def on_device(
    groups, cell_count, expression, dataset_id, dataset_map, sweep_count, picks,
    shared_init, specific_init,
):
    genes = expression.shape[0]
    rounds, per_round = picks.shape
    layers = cell_count // 2
    width = -(-genes // (cell_count * LANES)) * LANES
    cell = lax.axis_index("cell")
    limit = jnp.sum(
        jnp.where(jnp.arange(sweep_count.shape[0]) == dataset_map[0], sweep_count, 0)
    )
    mine = (cell % 2) * layers + cell // 2
    scalars = jnp.stack([limit, mine]).astype(jnp.int32)
    f32 = jnp.float32
    vmem = pl.BlockSpec(memory_space=pltpu.VMEM)
    loadings, stats, grams, shared, specific = pl.pallas_call(
        cell_kernel,
        out_shape=(
            jax.ShapeDtypeStruct((rounds, K, per_round), f32),
            jax.ShapeDtypeStruct((rounds, cell_count, K, width), f32),
            jax.ShapeDtypeStruct((rounds, K, LANES), f32),
            jax.ShapeDtypeStruct((K, width), f32),
            jax.ShapeDtypeStruct((K, width), f32),
        ),
        in_specs=[pl.BlockSpec(memory_space=pltpu.SMEM)] + [vmem] * 4,
        out_specs=(vmem,) * 5,
        scratch_shapes=[
            pltpu.VMEM((K, K, LANES), f32),
            pltpu.VMEM((K, width * cell_count), f32),
        ],
        compiler_params=pltpu.CompilerParams(vmem_limit_bytes=40 * 1024 * 1024),
        name="cells",
    )(scalars, expression, picks.reshape(1, rounds * per_round), shared_init, specific_init[0])
    dma = pltpu.SemaphoreType.DMA
    shared, specific = pl.pallas_call(
        functools.partial(basis_kernel, groups, cell_count),
        out_shape=(
            jax.ShapeDtypeStruct((K, genes), f32),
            jax.ShapeDtypeStruct((K, genes), f32),
        ),
        in_specs=[vmem] * 4,
        out_specs=(vmem,) * 2,
        scratch_shapes=[
            pltpu.VMEM((rounds, layers, K, width), f32),
            pltpu.VMEM((rounds, K, LANES), f32),
            pltpu.VMEM((rounds, layers, K, width + LANES), f32),
            pltpu.VMEM((rounds, layers - 1, K, width + LANES), f32),
            pltpu.VMEM((rounds, K, width + LANES), f32),
            pltpu.VMEM((rounds, groups - 1, K, width + LANES), f32),
            pltpu.VMEM((cell_count, K, width), f32),
            pltpu.VMEM((cell_count, K, width), f32),
            pltpu.VMEM((K, width), f32),
            pltpu.VMEM((K, LANES), f32),
            pltpu.VMEM((K, width), f32),
            pltpu.VMEM((K, width), f32),
            dma((rounds, 2)), dma((rounds, 2)),
            dma((rounds, layers - 1)), dma((rounds, layers - 1)),
            dma((rounds, groups - 1)), dma((rounds, groups - 1)),
            dma((2, layers - 1)), dma((2, layers - 1)),
            dma((2, layers)), dma((2, layers)),
        ],
        compiler_params=pltpu.CompilerParams(
            collective_id=0, has_side_effects=True, vmem_limit_bytes=40 * 1024 * 1024
        ),
        name="bases",
    )(stats, grams, shared, specific)
    return loadings, shared, specific[None]


def solution(mesh):
    return jax.shard_map(
        functools.partial(on_device, mesh.shape["grp"], mesh.shape["cell"]),
        mesh=mesh,
        in_specs=(
            P(None, ("grp", "cell")),
            P(("grp", "cell")),
            P("grp"),
            P(),
            P(None, ("grp", "cell")),
            P(),
            P("grp", None, None),
        ),
        out_specs=(P(None, None, ("grp", "cell")), P(), P("grp", None, None)),
        check_vma=False,
    )
```

```python
import functools

import jax
import jax.numpy as jnp
from jax import lax
from jax.experimental import pallas as pl
from jax.experimental.pallas import tpu as pltpu
from jax.sharding import PartitionSpec as P

K = 64
SWEEPS = 4
LANES = 128
BLOCK = 8

EPSILON = 1e-06
LAMBDA = 5.0
HIGHEST = lax.Precision.HIGHEST
MESH = pl.DeviceIdType.MESH
TRANSPOSED = (((1,), (1,)), ((), ()))


def identity_of(rows, columns):
    return (
        lax.broadcasted_iota(jnp.int32, (rows, columns), 0)
        == lax.broadcasted_iota(jnp.int32, (rows, columns), 1)
    ).astype(jnp.float32)


def cell_kernel(
    dataset_map, sweep_count, picks, expression_in, shared_in, specific_in,
    loadings_out, stats_out, grams_out, shared_out, specific_out,
    table, padded, expression, shared, specific, load_sem,
):
    rounds, chunks, _, width = stats_out.shape
    genes = shared.shape[1]
    pool = expression.shape[1]
    per_round = picks.shape[1]
    cells = per_round * rounds
    cell = lax.axis_index("cell")
    mine = (cell % 2) * (chunks // 2) + cell // 2

    loads = [
        pltpu.make_async_copy(source, place, load_sem.at[index])
        for index, (source, place) in enumerate(
            ((shared_in, shared), (specific_in.at[0], specific), (expression_in, expression))
        )
    ]
    for load in loads:
        load.start()
    padded[...] = jnp.zeros_like(padded)
    loads[0].wait()
    loads[1].wait()
    own = pl.ds(pl.multiple_of(mine * width, LANES), width)
    for source, place in ((shared, shared_out), (specific, specific_out)):
        padded[:, :genes] = source[...]
        place[...] = padded[:, own]

    combined = shared[...] + specific[...]
    gram = lax.dot_general(
        combined, combined, TRANSPOSED, precision=HIGHEST, preferred_element_type=jnp.float32
    ) + LAMBDA * lax.dot_general(
        specific[...], specific[...], TRANSPOSED, precision=HIGHEST,
        preferred_element_type=jnp.float32,
    )
    wanted = jnp.concatenate([picks[r : r + 1, :] for r in range(rounds)], axis=1)
    chosen = (
        lax.broadcasted_iota(jnp.int32, (pool, cells), 0) == wanted
    ).astype(jnp.bfloat16)
    loads[2].wait()
    data = jnp.dot(expression[...], chosen, preferred_element_type=jnp.float32).astype(jnp.bfloat16)
    target = jnp.dot(combined.astype(jnp.bfloat16), data, preferred_element_type=jnp.float32)

    eye = identity_of(K, K)
    divisor = jnp.sum(gram * eye, axis=1, keepdims=True) + EPSILON
    pull = eye - gram / divisor
    for factor in range(K):
        table[factor] = jnp.broadcast_to(pull[:, factor : factor + 1], (K, LANES))
    start = target / divisor
    blocks = K // BLOCK
    tiles = cells // LANES
    row = lax.broadcasted_iota(jnp.int32, (BLOCK, LANES), 0)

    limit = sweep_count[0]
    for index in range(1, sweep_count.shape[0]):
        limit = jnp.where(dataset_map[0] == index, sweep_count[index], limit)
    limits = jnp.full((BLOCK, LANES), limit, jnp.int32)

    def sweep(sweep_index, state):
        wish, held = [list(part) for part in state]
        active = limits > sweep_index
        for factor in range(K):
            block, place = divmod(factor, BLOCK)
            for tile in range(tiles):
                at = block * tiles + tile
                renewed = jnp.where(active, jnp.maximum(wish[at], 0.0), held[at])
                change = renewed - held[at]
                change = jnp.broadcast_to(change[place : place + 1], (BLOCK, LANES))
                held[at] = jnp.where(row == place, renewed, held[at])
                for other in range(blocks):
                    to = other * tiles + tile
                    wish[to] = (
                        wish[to]
                        + table[factor, other * BLOCK : (other + 1) * BLOCK, :] * change
                    )
        return tuple(wish), tuple(held)

    first = tuple(
        start[block * BLOCK : (block + 1) * BLOCK, tile * LANES : (tile + 1) * LANES]
        for block in range(blocks)
        for tile in range(tiles)
    )
    zero = tuple(jnp.zeros((BLOCK, LANES), jnp.float32) for _ in first)
    _, held = lax.fori_loop(0, SWEEPS, sweep, (first, zero))

    per_tile = per_round // LANES
    for round_index in range(rounds):
        parts = [
            jnp.concatenate([held[block * tiles + tile] for block in range(blocks)], axis=0)
            for tile in range(round_index * per_tile, (round_index + 1) * per_tile)
        ]
        loaded = parts[0] if per_tile == 1 else jnp.concatenate(parts, axis=1)
        loadings_out[round_index] = loaded
        grams_out[:, round_index * K : (round_index + 1) * K] = lax.dot_general(
            loaded, loaded, TRANSPOSED, precision=HIGHEST, preferred_element_type=jnp.float32
        )
        stats = lax.dot_general(
            loaded.astype(jnp.bfloat16),
            data[:, round_index * per_round : (round_index + 1) * per_round],
            TRANSPOSED,
            preferred_element_type=jnp.float32,
        )
        for chunk in range(chunks):
            low = chunk * width
            high = min(low + width, genes)
            if high < low + width:
                stats_out[round_index, chunk] = jnp.zeros((K, width), jnp.float32)
            if high > low:
                stats_out[round_index, chunk, :, : high - low] = stats[:, low:high]


def renew(current, residual, gram, scale, wish_ref, pull_ref, out_ref):
    width = current.shape[1]
    eye = identity_of(K, LANES)
    scaled = scale * gram
    divisor = jnp.maximum(jnp.sum(scaled * eye, axis=1, keepdims=True), 1.0)
    pull = eye - scaled / divisor
    wish_ref[...] = current + residual / divisor
    out_ref[...] = current
    row = lax.broadcasted_iota(jnp.int32, (BLOCK, width), 0)

    def step(block, carry):
        turned = pltpu.roll(pull, LANES - BLOCK * block, axis=1)
        pull_ref[...] = turned
        rows = pl.ds(pl.multiple_of(block * BLOCK, BLOCK), BLOCK)
        near = pull_ref[rows, :]
        wish = wish_ref[rows, :]
        held = out_ref[rows, :]
        total = wish_ref[...]
        for place in range(BLOCK):
            renewed = jnp.maximum(wish, 0.0)
            change = jnp.broadcast_to((renewed - held)[place : place + 1], (BLOCK, width))
            held = jnp.where(row == place, renewed, held)
            wish = wish + jnp.broadcast_to(near[:, place : place + 1], (BLOCK, width)) * change
            wide = jnp.concatenate([change] * (K // BLOCK), axis=0)
            total = total + jnp.broadcast_to(turned[:, place : place + 1], (K, width)) * wide
        wish_ref[...] = total
        out_ref[rows, :] = held
        return carry

    lax.fori_loop(0, K // BLOCK, step, 0)


def plus(total, increase):
    return increase if total is None else total + increase


def gram_of(packed, index):
    tile, offset = divmod(index * K, LANES)
    piece = packed[:, tile * LANES : (tile + 1) * LANES]
    if offset:
        piece = pltpu.roll(piece, LANES - offset, axis=1)
    lane = lax.broadcasted_iota(jnp.int32, (K, LANES), 1)
    return jnp.where(lane < K, piece, 0.0)


def basis_kernel(
    groups, cell_count, stats, grams, shared, specific, shared_out, specific_out,
    sib_stats, sib_grams, along, arrived, gram_along, gram_arrived,
    sent, gathered, gram_sent, gram_gathered, wide_shared, wide_specific,
    wish_ref, pull_ref, shared_ref, specific_ref,
    sib_send, sib_recv, along_send, along_recv, grp_send, grp_recv,
    out_send, out_recv, pair_send, pair_recv, part_send, part_recv,
):
    rounds, chunks, _, width = stats.shape
    layers = cell_count // 2
    grp = lax.axis_index("grp")
    cell = lax.axis_index("cell")
    layer = cell // 2
    core = cell % 2
    sibling = layer * 2 + (1 - core)
    mine = core * layers + layer
    share = K // groups
    own_rows = pl.ds(pl.multiple_of(grp * share, BLOCK), share)

    def layer_at(offset):
        return (layer + offset) % layers

    barrier = pltpu.get_barrier_semaphore()
    pl.semaphore_wait(barrier, 1 + (layers - 1) + (groups - 1))

    started = []

    def send(source, place, send_sem, recv_sem, device):
        copy = pltpu.make_async_remote_copy(
            src_ref=source, dst_ref=place, send_sem=send_sem, recv_sem=recv_sem,
            device_id=device, device_id_type=MESH,
        )
        copy.start()
        started.append(copy)
        return copy

    gram_pair = send(
        grams, sib_grams, sib_send.at[rounds], sib_recv.at[rounds], {"cell": sibling}
    )
    pair = [
        send(
            stats.at[r, pl.ds((1 - core) * layers, layers)], sib_stats.at[r],
            sib_send.at[r], sib_recv.at[r], {"cell": sibling},
        )
        for r in range(rounds)
    ]
    gram_pair.wait_recv()
    gram_along[...] = grams[...] + sib_grams[...]
    gram_across = [
        send(
            gram_along, gram_arrived.at[offset - 1],
            along_send.at[rounds, offset - 1], along_recv.at[rounds, offset - 1],
            {"cell": layer_at(offset) * 2 + core},
        )
        for offset in range(layers - 1, 0, -1)
    ]
    across = []
    for r in range(rounds):
        pair[r].wait_recv()
        copies = []
        for offset in range(layers - 1, -1, -1):
            at = layer_at(offset)
            along[r, offset] = stats[r, core * layers + at] + sib_stats[r, at]
            if offset:
                copies.append(send(
                    along.at[r, offset], arrived.at[r, offset - 1],
                    along_send.at[r, offset - 1], along_recv.at[r, offset - 1],
                    {"cell": at * 2 + core},
                ))
        across.append(copies)
    for copy in gram_across:
        copy.wait_recv()
    gram_sum = gram_along[...]
    for offset in range(1, layers):
        gram_sum = gram_sum + gram_arrived[offset - 1]
    gram_sent[...] = gram_sum
    gram_copies = [
        send(
            gram_sent, gram_gathered.at[offset - 1], grp_send.at[rounds, offset - 1],
            grp_recv.at[rounds, offset - 1], {"grp": (grp + offset) % groups},
        )
        for offset in range(1, groups)
    ]

    shared_ref[...] = shared[...]
    specific_ref[...] = specific[...]
    stat = gram = gram_total = None
    gram_groups = None
    for r in range(rounds):
        for copy in across[r]:
            copy.wait_recv()
        increase = along[r, 0]
        for offset in range(1, layers):
            increase = increase + arrived[r, offset - 1]
        stat = plus(stat, increase)
        gram = plus(gram, gram_of(gram_sum, r))
        small = gram[:, :K]
        before = specific_ref[...]
        pulled = jnp.dot(small, before, precision=HIGHEST, preferred_element_type=jnp.float32)
        sent[r] = stat - pulled
        copies = [
            send(sent.at[r], gathered.at[r, offset - 1], grp_send.at[r, offset - 1],
                 grp_recv.at[r, offset - 1], {"grp": (grp + offset) % groups})
            for offset in range(1, groups)
        ]
        if gram_groups is None:
            for copy in gram_copies:
                copy.wait_recv()
            gram_groups = gram_sum
            for offset in range(1, groups):
                gram_groups = gram_groups + gram_gathered[offset - 1]
        gram_total = plus(gram_total, gram_of(gram_groups, r))
        for copy in copies:
            copy.wait_recv()
        carried = sent[r]
        for offset in range(1, groups):
            carried = carried + gathered[r, offset - 1]
        old = shared_ref[...]
        residual = carried - jnp.dot(
            gram_total[:, :K], old, precision=HIGHEST, preferred_element_type=jnp.float32
        )
        renew(old, residual, gram_total, 1.0, wish_ref, pull_ref, shared_ref)
        last = r == rounds - 1
        if last:
            wide_shared[mine] = shared_ref[...]
            shared_copies = spread(
                send, wide_shared, 0, mine, own_rows, core, layers, layer_at, sibling,
                out_send, out_recv, pair_send, pair_recv,
            )
        residual = stat - (1.0 + LAMBDA) * pulled - jnp.dot(
            small, shared_ref[...], precision=HIGHEST, preferred_element_type=jnp.float32
        )
        renew(before, residual, gram, 1.0 + LAMBDA, wish_ref, pull_ref, specific_ref)
        if last:
            wide_specific[mine] = specific_ref[...]
            specific_copies = spread(
                send, wide_specific, 1, mine, pl.ds(0, K), core, layers, layer_at, sibling,
                out_send, out_recv, pair_send, pair_recv,
            )

    fetched_shared, fetched_specific = [shared_copies[0]], [specific_copies[0]]
    parts = {}
    for offset in range(1, layers):
        came = core * layers + layer_at(layers - offset)
        shared_copies[offset].wait_recv()
        parts[offset] = [
            send(
                wide_shared.at[came, own_rows], wide_shared.at[came, own_rows],
                part_send.at[offset - 1, other - 1], part_recv.at[offset - 1, other - 1],
                {"grp": (grp + other) % groups},
            )
            for other in range(1, groups)
        ]

    def pass_on(wide, index, offset):
        came = core * layers + layer_at(layers - offset)
        return send(
            wide.at[came], wide.at[came], pair_send.at[index, offset],
            pair_recv.at[index, offset], {"cell": sibling},
        )

    for offset in range(1, layers):
        for copy in parts[offset]:
            copy.wait_recv()
        fetched_shared.append(pass_on(wide_shared, 0, offset))
    for offset in range(1, layers):
        specific_copies[offset].wait_recv()
        fetched_specific.append(pass_on(wide_specific, 1, offset))
    genes = shared_out.shape[1]
    for wide, fetched, out in (
        (wide_shared, fetched_shared, shared_out),
        (wide_specific, fetched_specific, specific_out),
    ):
        for copy in fetched:
            copy.wait_recv()
        for chunk in range(chunks):
            low = chunk * width
            high = min(low + width, genes)
            if high > low:
                out[:, low:high] = wide[chunk, :, : high - low]
    for copy in started:
        copy.wait_send()


def spread(
    send, wide, index, mine, rows, core, layers, layer_at, sibling,
    out_send, out_recv, pair_send, pair_recv,
):
    copies = {}
    for offset in range(layers - 1, 0, -1):
        copies[offset] = send(
            wide.at[mine, rows], wide.at[mine, rows], out_send.at[index, offset - 1],
            out_recv.at[index, offset - 1], {"cell": layer_at(offset) * 2 + core},
        )
    copies[0] = send(
        wide.at[mine], wide.at[mine], pair_send.at[index, 0], pair_recv.at[index, 0],
        {"cell": sibling},
    )
    return copies


def round_kernel(groups, cell_count, *refs):
    (dataset_map, sweep_count, picks, expression_in, shared_in, specific_in,
     loadings_out, shared_out, specific_out,
     stats, grams, shared_own, specific_own, *rest) = refs
    local, remote = rest[:6], rest[6:]
    layers = cell_count // 2
    grp = lax.axis_index("grp")
    cell = lax.axis_index("cell")
    layer = cell // 2
    core = cell % 2
    sibling = layer * 2 + (1 - core)
    barrier = pltpu.get_barrier_semaphore()
    pl.semaphore_signal(barrier, inc=1, device_id={"cell": sibling}, device_id_type=MESH)
    for offset in range(1, layers):
        pl.semaphore_signal(
            barrier, inc=1, device_id={"cell": (layer + offset) % layers * 2 + core}, device_id_type=MESH
        )
    for offset in range(1, groups):
        pl.semaphore_signal(
            barrier, inc=1, device_id={"grp": (grp + offset) % groups}, device_id_type=MESH
        )
    cell_kernel(
        dataset_map, sweep_count, picks, expression_in, shared_in, specific_in,
        loadings_out, stats, grams, shared_own, specific_own, *local,
    )
    basis_kernel(
        groups, cell_count, stats, grams, shared_own, specific_own,
        shared_out, specific_out, *remote,
    )


def on_device(
    groups, cell_count, expression, dataset_id, dataset_map, sweep_count, picks,
    shared_init, specific_init,
):
    genes = expression.shape[0]
    rounds, per_round = picks.shape
    layers = cell_count // 2
    width = -(-genes // (cell_count * LANES)) * LANES
    f32 = jnp.float32
    vmem = pl.BlockSpec(memory_space=pltpu.VMEM)
    smem = pl.BlockSpec(memory_space=pltpu.SMEM)
    hbm = pl.BlockSpec(memory_space=pltpu.HBM)
    packed = -(-rounds * K // LANES) * LANES
    dma = pltpu.SemaphoreType.DMA
    loadings, shared, specific = pl.pallas_call(
        functools.partial(round_kernel, groups, cell_count),
        out_shape=(
            jax.ShapeDtypeStruct((rounds, K, per_round), f32),
            jax.ShapeDtypeStruct((K, genes), f32),
            jax.ShapeDtypeStruct((K, genes), f32),
        ),
        in_specs=[smem, smem, vmem, hbm, hbm, hbm],
        out_specs=(vmem,) * 3,
        scratch_shapes=[
            pltpu.VMEM((rounds, cell_count, K, width), f32),
            pltpu.VMEM((K, packed), f32),
            pltpu.VMEM((K, width), f32),
            pltpu.VMEM((K, width), f32),
            pltpu.VMEM((K, K, LANES), f32),
            pltpu.VMEM((K, width * cell_count), f32),
            pltpu.VMEM(expression.shape, expression.dtype),
            pltpu.VMEM((K, genes), f32),
            pltpu.VMEM((K, genes), f32),
            dma((3,)),
            pltpu.VMEM((rounds, layers, K, width), f32),
            pltpu.VMEM((K, packed), f32),
            pltpu.VMEM((rounds, layers, K, width), f32),
            pltpu.VMEM((rounds, layers - 1, K, width), f32),
            pltpu.VMEM((K, packed), f32),
            pltpu.VMEM((layers - 1, K, packed), f32),
            pltpu.VMEM((rounds, K, width), f32),
            pltpu.VMEM((rounds, groups - 1, K, width), f32),
            pltpu.VMEM((K, packed), f32),
            pltpu.VMEM((groups - 1, K, packed), f32),
            pltpu.VMEM((cell_count, K, width), f32),
            pltpu.VMEM((cell_count, K, width), f32),
            pltpu.VMEM((K, width), f32),
            pltpu.VMEM((K, LANES), f32),
            pltpu.VMEM((K, width), f32),
            pltpu.VMEM((K, width), f32),
            dma((rounds + 1,)), dma((rounds + 1,)),
            dma((rounds + 1, layers - 1)), dma((rounds + 1, layers - 1)),
            dma((rounds + 1, groups - 1)), dma((rounds + 1, groups - 1)),
            dma((2, layers - 1)), dma((2, layers - 1)),
            dma((2, layers)), dma((2, layers)),
            dma((layers - 1, groups - 1)), dma((layers - 1, groups - 1)),
        ],
        compiler_params=pltpu.CompilerParams(
            collective_id=0, has_side_effects=True, vmem_limit_bytes=62 * 1024 * 1024
        ),
        name="rounds",
    )(dataset_map, sweep_count, picks, expression, shared_init, specific_init)
    return loadings, shared, specific[None]


def solution(mesh):
    return jax.shard_map(
        functools.partial(on_device, mesh.shape["grp"], mesh.shape["cell"]),
        mesh=mesh,
        in_specs=(
            P(None, ("grp", "cell")),
            P(("grp", "cell")),
            P("grp"),
            P(),
            P(None, ("grp", "cell")),
            P(),
            P("grp", None, None),
        ),
        out_specs=(P(None, None, ("grp", "cell")), P(), P("grp", None, None)),
        check_vma=False,
    )
```

```python
import functools

import jax
import jax.numpy as jnp
from jax import lax
from jax.experimental import pallas as pl
from jax.experimental.pallas import tpu as pltpu
from jax.sharding import PartitionSpec as P

K = 64
SWEEPS = 4
LANES = 128
BLOCK = 8

EPSILON = 1e-06
LAMBDA = 5.0
HIGHEST = lax.Precision.HIGHEST
MESH = pl.DeviceIdType.MESH
TRANSPOSED = (((1,), (1,)), ((), ()))


def identity_of(rows, columns):
    return (
        lax.broadcasted_iota(jnp.int32, (rows, columns), 0)
        == lax.broadcasted_iota(jnp.int32, (rows, columns), 1)
    ).astype(jnp.float32)


def cell_kernel(
    dataset_map, sweep_count, picks, expression_in, shared_in, specific_in,
    loadings_out, stats_out, grams_out, shared_out, specific_out,
    table, padded, expression, shared, specific, load_sem,
):
    rounds, chunks, _, width = stats_out.shape
    genes = shared.shape[1]
    pool = expression.shape[1]
    per_round = picks.shape[1]
    cells = per_round * rounds
    cell = lax.axis_index("cell")
    mine = (cell % 2) * (chunks // 2) + cell // 2

    loads = [
        pltpu.make_async_copy(source, place, load_sem.at[index])
        for index, (source, place) in enumerate(
            ((shared_in, shared), (specific_in.at[0], specific), (expression_in, expression))
        )
    ]
    for load in loads:
        load.start()
    padded[...] = jnp.zeros_like(padded)
    loads[0].wait()
    loads[1].wait()
    own = pl.ds(pl.multiple_of(mine * width, LANES), width)
    for source, place in ((shared, shared_out), (specific, specific_out)):
        padded[:, :genes] = source[...]
        place[...] = padded[:, own]

    combined = shared[...] + specific[...]
    gram = lax.dot_general(
        combined, combined, TRANSPOSED, precision=HIGHEST, preferred_element_type=jnp.float32
    ) + LAMBDA * lax.dot_general(
        specific[...], specific[...], TRANSPOSED, precision=HIGHEST,
        preferred_element_type=jnp.float32,
    )
    wanted = jnp.concatenate([picks[r : r + 1, :] for r in range(rounds)], axis=1)
    chosen = (
        lax.broadcasted_iota(jnp.int32, (pool, cells), 0) == wanted
    ).astype(jnp.bfloat16)
    loads[2].wait()
    data = jnp.dot(expression[...], chosen, preferred_element_type=jnp.float32).astype(jnp.bfloat16)
    target = jnp.dot(combined.astype(jnp.bfloat16), data, preferred_element_type=jnp.float32)

    eye = identity_of(K, K)
    divisor = jnp.sum(gram * eye, axis=1, keepdims=True) + EPSILON
    pull = eye - gram / divisor
    for factor in range(K):
        table[factor] = jnp.broadcast_to(pull[:, factor : factor + 1], (K, LANES))
    start = target / divisor
    blocks = K // BLOCK
    tiles = cells // LANES
    row = lax.broadcasted_iota(jnp.int32, (BLOCK, LANES), 0)

    limit = sweep_count[0]
    for index in range(1, sweep_count.shape[0]):
        limit = jnp.where(dataset_map[0] == index, sweep_count[index], limit)
    limits = jnp.full((BLOCK, LANES), limit, jnp.int32)

    def sweep(sweep_index, state):
        wish, held = [list(part) for part in state]
        active = limits > sweep_index
        for factor in range(K):
            block, place = divmod(factor, BLOCK)
            for tile in range(tiles):
                at = block * tiles + tile
                renewed = jnp.where(active, jnp.maximum(wish[at], 0.0), held[at])
                change = renewed - held[at]
                change = jnp.broadcast_to(change[place : place + 1], (BLOCK, LANES))
                held[at] = jnp.where(row == place, renewed, held[at])
                for other in range(blocks):
                    to = other * tiles + tile
                    wish[to] = (
                        wish[to]
                        + table[factor, other * BLOCK : (other + 1) * BLOCK, :] * change
                    )
        return tuple(wish), tuple(held)

    first = tuple(
        start[block * BLOCK : (block + 1) * BLOCK, tile * LANES : (tile + 1) * LANES]
        for block in range(blocks)
        for tile in range(tiles)
    )
    zero = tuple(jnp.zeros((BLOCK, LANES), jnp.float32) for _ in first)
    _, held = lax.fori_loop(0, SWEEPS, sweep, (first, zero))

    per_tile = per_round // LANES
    for round_index in range(rounds):
        parts = [
            jnp.concatenate([held[block * tiles + tile] for block in range(blocks)], axis=0)
            for tile in range(round_index * per_tile, (round_index + 1) * per_tile)
        ]
        loaded = parts[0] if per_tile == 1 else jnp.concatenate(parts, axis=1)
        loadings_out[round_index] = loaded
        grams_out[:, round_index * K : (round_index + 1) * K] = lax.dot_general(
            loaded, loaded, TRANSPOSED, precision=HIGHEST, preferred_element_type=jnp.float32
        )
        stats = lax.dot_general(
            loaded.astype(jnp.bfloat16),
            data[:, round_index * per_round : (round_index + 1) * per_round],
            TRANSPOSED,
            preferred_element_type=jnp.float32,
        )
        for chunk in range(chunks):
            low = chunk * width
            high = min(low + width, genes)
            if high < low + width:
                stats_out[round_index, chunk] = jnp.zeros((K, width), jnp.float32)
            if high > low:
                stats_out[round_index, chunk, :, : high - low] = stats[:, low:high]


def renew(current, residual, gram, scale, wish_ref, pull_ref, out_ref):
    width = current.shape[1]
    eye = identity_of(K, LANES)
    scaled = scale * gram
    divisor = jnp.maximum(jnp.sum(scaled * eye, axis=1, keepdims=True), 1.0)
    pull = eye - scaled / divisor
    wish_ref[...] = current + residual / divisor
    out_ref[...] = current
    row = lax.broadcasted_iota(jnp.int32, (BLOCK, width), 0)

    def step(block, carry):
        turned = pltpu.roll(pull, LANES - BLOCK * block, axis=1)
        pull_ref[...] = turned
        rows = pl.ds(pl.multiple_of(block * BLOCK, BLOCK), BLOCK)
        near = pull_ref[rows, :]
        wish = wish_ref[rows, :]
        held = out_ref[rows, :]
        total = wish_ref[...]
        for place in range(BLOCK):
            renewed = jnp.maximum(wish, 0.0)
            change = jnp.broadcast_to((renewed - held)[place : place + 1], (BLOCK, width))
            held = jnp.where(row == place, renewed, held)
            wish = wish + jnp.broadcast_to(near[:, place : place + 1], (BLOCK, width)) * change
            wide = jnp.concatenate([change] * (K // BLOCK), axis=0)
            total = total + jnp.broadcast_to(turned[:, place : place + 1], (K, width)) * wide
        wish_ref[...] = total
        out_ref[rows, :] = held
        return carry

    lax.fori_loop(0, K // BLOCK, step, 0)


def plus(total, increase):
    return increase if total is None else total + increase


def gram_of(packed, index):
    tile, offset = divmod(index * K, LANES)
    piece = packed[:, tile * LANES : (tile + 1) * LANES]
    if offset:
        piece = pltpu.roll(piece, LANES - offset, axis=1)
    lane = lax.broadcasted_iota(jnp.int32, (K, LANES), 1)
    return jnp.where(lane < K, piece, 0.0)


def basis_kernel(
    groups, cell_count, stats, grams, shared, specific, shared_out, specific_out,
    sib_stats, sib_grams, along, arrived, gram_along, gram_arrived,
    sent, gathered, gram_sent, gram_gathered, wide_shared, wide_specific,
    wish_ref, pull_ref, shared_ref, specific_ref,
    sib_send, sib_recv, along_send, along_recv, grp_send, grp_recv,
    out_send, out_recv, pair_send, pair_recv, part_send, part_recv,
):
    rounds, chunks, _, width = stats.shape
    layers = cell_count // 2
    grp = lax.axis_index("grp")
    cell = lax.axis_index("cell")
    layer = cell // 2
    core = cell % 2
    sibling = layer * 2 + (1 - core)
    mine = core * layers + layer
    share = K // groups
    own_rows = pl.ds(pl.multiple_of(grp * share, BLOCK), share)

    def layer_at(offset):
        return (layer + offset) % layers

    barrier = pltpu.get_barrier_semaphore()
    pl.semaphore_wait(barrier, 1 + (layers - 1) + (groups - 1))

    started = []

    def send(source, place, send_sem, recv_sem, device):
        copy = pltpu.make_async_remote_copy(
            src_ref=source, dst_ref=place, send_sem=send_sem, recv_sem=recv_sem,
            device_id=device, device_id_type=MESH,
        )
        copy.start()
        started.append(copy)
        return copy

    gram_pair = send(
        grams, sib_grams, sib_send.at[rounds], sib_recv.at[rounds], {"cell": sibling}
    )
    pair = [
        send(
            stats.at[r, pl.ds((1 - core) * layers, layers)], sib_stats.at[r],
            sib_send.at[r], sib_recv.at[r], {"cell": sibling},
        )
        for r in range(rounds)
    ]
    gram_pair.wait_recv()
    gram_along[...] = grams[...] + sib_grams[...]
    gram_across = [
        send(
            gram_along, gram_arrived.at[offset - 1],
            along_send.at[rounds, offset - 1], along_recv.at[rounds, offset - 1],
            {"cell": layer_at(offset) * 2 + core},
        )
        for offset in range(layers - 1, 0, -1)
    ]
    across = []
    for r in range(rounds):
        pair[r].wait_recv()
        copies = []
        for offset in range(layers - 1, -1, -1):
            at = layer_at(offset)
            along[r, offset] = stats[r, core * layers + at] + sib_stats[r, at]
            if offset:
                copies.append(send(
                    along.at[r, offset], arrived.at[r, offset - 1],
                    along_send.at[r, offset - 1], along_recv.at[r, offset - 1],
                    {"cell": at * 2 + core},
                ))
        across.append(copies)
    for copy in gram_across:
        copy.wait_recv()
    gram_sum = gram_along[...]
    for offset in range(1, layers):
        gram_sum = gram_sum + gram_arrived[offset - 1]
    gram_sent[...] = gram_sum
    gram_copies = [
        send(
            gram_sent, gram_gathered.at[offset - 1], grp_send.at[rounds, offset - 1],
            grp_recv.at[rounds, offset - 1], {"grp": (grp + offset) % groups},
        )
        for offset in range(1, groups)
    ]

    shared_ref[...] = shared[...]
    specific_ref[...] = specific[...]
    stat = gram = gram_total = None
    gram_groups = None
    for r in range(rounds):
        for copy in across[r]:
            copy.wait_recv()
        increase = along[r, 0]
        for offset in range(1, layers):
            increase = increase + arrived[r, offset - 1]
        stat = plus(stat, increase)
        gram = plus(gram, gram_of(gram_sum, r))
        small = gram[:, :K]
        before = specific_ref[...]
        pulled = jnp.dot(small, before, precision=HIGHEST, preferred_element_type=jnp.float32)
        sent[r] = stat - pulled
        copies = [
            send(sent.at[r], gathered.at[r, offset - 1], grp_send.at[r, offset - 1],
                 grp_recv.at[r, offset - 1], {"grp": (grp + offset) % groups})
            for offset in range(1, groups)
        ]
        if gram_groups is None:
            for copy in gram_copies:
                copy.wait_recv()
            gram_groups = gram_sum
            for offset in range(1, groups):
                gram_groups = gram_groups + gram_gathered[offset - 1]
        gram_total = plus(gram_total, gram_of(gram_groups, r))
        old = shared_ref[...]
        expected = jnp.dot(
            gram_total[:, :K], old, precision=HIGHEST, preferred_element_type=jnp.float32
        )
        for copy in copies:
            copy.wait_recv()
        carried = sent[r]
        for offset in range(1, groups):
            carried = carried + gathered[r, offset - 1]
        residual = carried - expected
        renew(old, residual, gram_total, 1.0, wish_ref, pull_ref, shared_ref)
        last = r == rounds - 1
        if last:
            wide_shared[mine] = shared_ref[...]
            shared_copies = spread(
                send, wide_shared, 0, mine, own_rows, core, layers, layer_at, sibling,
                out_send, out_recv, pair_send, pair_recv,
            )
        residual = stat - (1.0 + LAMBDA) * pulled - jnp.dot(
            small, shared_ref[...], precision=HIGHEST, preferred_element_type=jnp.float32
        )
        renew(before, residual, gram, 1.0 + LAMBDA, wish_ref, pull_ref, specific_ref)
        if last:
            wide_specific[mine] = specific_ref[...]
            specific_copies = spread(
                send, wide_specific, 1, mine, pl.ds(0, K), core, layers, layer_at, sibling,
                out_send, out_recv, pair_send, pair_recv,
            )

    fetched_shared, fetched_specific = [shared_copies[0]], [specific_copies[0]]
    parts = {}
    for offset in range(1, layers):
        came = core * layers + layer_at(layers - offset)
        shared_copies[offset].wait_recv()
        parts[offset] = [
            send(
                wide_shared.at[came, own_rows], wide_shared.at[came, own_rows],
                part_send.at[offset - 1, other - 1], part_recv.at[offset - 1, other - 1],
                {"grp": (grp + other) % groups},
            )
            for other in range(1, groups)
        ]

    def pass_on(wide, index, offset):
        came = core * layers + layer_at(layers - offset)
        return send(
            wide.at[came], wide.at[came], pair_send.at[index, offset],
            pair_recv.at[index, offset], {"cell": sibling},
        )

    for offset in range(1, layers):
        for copy in parts[offset]:
            copy.wait_recv()
        fetched_shared.append(pass_on(wide_shared, 0, offset))
    for offset in range(1, layers):
        specific_copies[offset].wait_recv()
        fetched_specific.append(pass_on(wide_specific, 1, offset))
    genes = shared_out.shape[1]
    for wide, fetched, out in (
        (wide_shared, fetched_shared, shared_out),
        (wide_specific, fetched_specific, specific_out),
    ):
        for copy in fetched:
            copy.wait_recv()
        for chunk in range(chunks):
            low = chunk * width
            high = min(low + width, genes)
            if high > low:
                out[:, low:high] = wide[chunk, :, : high - low]
    for copy in started:
        copy.wait_send()


def spread(
    send, wide, index, mine, rows, core, layers, layer_at, sibling,
    out_send, out_recv, pair_send, pair_recv,
):
    copies = {}
    for offset in range(layers - 1, 0, -1):
        copies[offset] = send(
            wide.at[mine, rows], wide.at[mine, rows], out_send.at[index, offset - 1],
            out_recv.at[index, offset - 1], {"cell": layer_at(offset) * 2 + core},
        )
    copies[0] = send(
        wide.at[mine], wide.at[mine], pair_send.at[index, 0], pair_recv.at[index, 0],
        {"cell": sibling},
    )
    return copies


def round_kernel(groups, cell_count, *refs):
    (dataset_map, sweep_count, picks, expression_in, shared_in, specific_in,
     loadings_out, shared_out, specific_out,
     stats, grams, shared_own, specific_own, *rest) = refs
    local, remote = rest[:6], rest[6:]
    layers = cell_count // 2
    grp = lax.axis_index("grp")
    cell = lax.axis_index("cell")
    layer = cell // 2
    core = cell % 2
    sibling = layer * 2 + (1 - core)
    barrier = pltpu.get_barrier_semaphore()
    pl.semaphore_signal(barrier, inc=1, device_id={"cell": sibling}, device_id_type=MESH)
    for offset in range(1, layers):
        pl.semaphore_signal(
            barrier, inc=1, device_id={"cell": (layer + offset) % layers * 2 + core}, device_id_type=MESH
        )
    for offset in range(1, groups):
        pl.semaphore_signal(
            barrier, inc=1, device_id={"grp": (grp + offset) % groups}, device_id_type=MESH
        )
    cell_kernel(
        dataset_map, sweep_count, picks, expression_in, shared_in, specific_in,
        loadings_out, stats, grams, shared_own, specific_own, *local,
    )
    basis_kernel(
        groups, cell_count, stats, grams, shared_own, specific_own,
        shared_out, specific_out, *remote,
    )


def on_device(
    groups, cell_count, expression, dataset_id, dataset_map, sweep_count, picks,
    shared_init, specific_init,
):
    genes = expression.shape[0]
    rounds, per_round = picks.shape
    layers = cell_count // 2
    width = -(-genes // (cell_count * LANES)) * LANES
    f32 = jnp.float32
    vmem = pl.BlockSpec(memory_space=pltpu.VMEM)
    smem = pl.BlockSpec(memory_space=pltpu.SMEM)
    hbm = pl.BlockSpec(memory_space=pltpu.HBM)
    packed = -(-rounds * K // LANES) * LANES
    dma = pltpu.SemaphoreType.DMA
    loadings, shared, specific = pl.pallas_call(
        functools.partial(round_kernel, groups, cell_count),
        out_shape=(
            jax.ShapeDtypeStruct((rounds, K, per_round), f32),
            jax.ShapeDtypeStruct((K, genes), f32),
            jax.ShapeDtypeStruct((K, genes), f32),
        ),
        in_specs=[smem, smem, vmem, hbm, hbm, hbm],
        out_specs=(vmem,) * 3,
        scratch_shapes=[
            pltpu.VMEM((rounds, cell_count, K, width), f32),
            pltpu.VMEM((K, packed), f32),
            pltpu.VMEM((K, width), f32),
            pltpu.VMEM((K, width), f32),
            pltpu.VMEM((K, K, LANES), f32),
            pltpu.VMEM((K, width * cell_count), f32),
            pltpu.VMEM(expression.shape, expression.dtype),
            pltpu.VMEM((K, genes), f32),
            pltpu.VMEM((K, genes), f32),
            dma((3,)),
            pltpu.VMEM((rounds, layers, K, width), f32),
            pltpu.VMEM((K, packed), f32),
            pltpu.VMEM((rounds, layers, K, width), f32),
            pltpu.VMEM((rounds, layers - 1, K, width), f32),
            pltpu.VMEM((K, packed), f32),
            pltpu.VMEM((layers - 1, K, packed), f32),
            pltpu.VMEM((rounds, K, width), f32),
            pltpu.VMEM((rounds, groups - 1, K, width), f32),
            pltpu.VMEM((K, packed), f32),
            pltpu.VMEM((groups - 1, K, packed), f32),
            pltpu.VMEM((cell_count, K, width), f32),
            pltpu.VMEM((cell_count, K, width), f32),
            pltpu.VMEM((K, width), f32),
            pltpu.VMEM((K, LANES), f32),
            pltpu.VMEM((K, width), f32),
            pltpu.VMEM((K, width), f32),
            dma((rounds + 1,)), dma((rounds + 1,)),
            dma((rounds + 1, layers - 1)), dma((rounds + 1, layers - 1)),
            dma((rounds + 1, groups - 1)), dma((rounds + 1, groups - 1)),
            dma((2, layers - 1)), dma((2, layers - 1)),
            dma((2, layers)), dma((2, layers)),
            dma((layers - 1, groups - 1)), dma((layers - 1, groups - 1)),
        ],
        compiler_params=pltpu.CompilerParams(
            collective_id=0, has_side_effects=True, vmem_limit_bytes=62 * 1024 * 1024
        ),
        name="rounds",
    )(dataset_map, sweep_count, picks, expression, shared_init, specific_init)
    return loadings, shared, specific[None]


def solution(mesh):
    return jax.shard_map(
        functools.partial(on_device, mesh.shape["grp"], mesh.shape["cell"]),
        mesh=mesh,
        in_specs=(
            P(None, ("grp", "cell")),
            P(("grp", "cell")),
            P("grp"),
            P(),
            P(None, ("grp", "cell")),
            P(),
            P("grp", None, None),
        ),
        out_specs=(P(None, None, ("grp", "cell")), P(), P("grp", None, None)),
        check_vma=False,
    )
```
